256 devices in a mesh: island: 16 (over y, z_lo), fsdp: 16 (over z_hi, x, core).
Axes of the slice: x: 4, y: 4, z: 8 (z_hi: 2, z_lo: 4; z = z_hi * 4 + z_lo), core: 2. Of those that a mesh axis runs over, the one named last changes fastest.
Arguments:
- acts: bfloat16 [131072, 832], P(('island', 'fsdp')), may hold values from -6 to 6
- grad_out: bfloat16 [131072, 4096], P(('island', 'fsdp')), may hold values from -6 to 6
- next_acts: bfloat16 [131072, 832], P(('island', 'fsdp')), may hold values from -6 to 6
- inner_params: float32 [16, 4096, 832], P('island', 'fsdp'), may hold values from -0.2 to 0.2
- adam_first: float32 [16, 4096, 832], P('island', 'fsdp'), may hold values from -0.06 to 0.06
- adam_second: float32 [16, 4096, 832], P('island', 'fsdp'), may hold values from 1e-06 to 0.001
- base_params: float32 [4096, 832], P('fsdp'), may hold values from -0.21875 to 0.21875
- outer_moment: float32 [4096, 832], P('fsdp'), may hold values from -0.06 to 0.06
Outputs:
- new_base: float32 [4096, 832], P('fsdp', 'island')
- new_moment: float32 [4096, 832], P('fsdp', 'island')
- next_out: bfloat16 [131072, 4096], P(('island', 'fsdp'))
The draws below stay inside these ranges and needn't reach their ends.
All inputs are finite; a program needn't handle non-finite values.
Results may differ from the reference program's by a relative error of at most 0.005.
Values may be sent and summed in bfloat16 or wider, within the bound.
A program may use at most 128 MiB of HBM per device.

```python
import math
import jax
import jax.numpy as jnp
from jax import lax

D = 832
FF = 4096
TOK_DEV = 512
INNER_STEP = 500
TOKENS = 131072
REPLICAS = 16
N_ISLAND = 16
N_FSDP = 16


def shard_levels(rng, shape, shards, least, largest):
    factor_of = 1.0
    for position, blocks in shards:
        steps = jax.random.uniform(jax.random.fold_in(jax.random.fold_in(rng, 6), position), (blocks,), jnp.float32, least / len(shards), largest / len(shards))
        factor_of = factor_of * jnp.repeat(jnp.exp(steps), shape[position] // blocks).reshape((-1,) + (1,) * (len(shape) - 1 - position))
    return factor_of


def bell_draw(rng, shape, spread, bound, cuts=(), kind=jnp.bfloat16):
    entries = spread * jax.random.normal(rng, shape, jnp.float32)
    if cuts:
        entries = entries * shard_levels(rng, shape, cuts, -0.22, 0.18)
    return jnp.clip(entries, -bound, bound).astype(kind)


def setup_inputs(seed: int = 0) -> dict:
    arg_keys = jax.random.split(jax.random.key(seed), 9)
    acts = bell_draw(arg_keys[0], (TOKENS, D), 1.0, 6.0, ((0, 256),))
    grad_out = bell_draw(arg_keys[1], (TOKENS, FF), 1.0, 6.0, ((0, 256),))
    next_acts = bell_draw(arg_keys[2], (TOKENS, D), 1.0, 6.0, ((0, 256),))
    inner_params = bell_draw(arg_keys[3], (REPLICAS, FF, D), 0.035, 0.2, ((0, 16), (1, 16)), jnp.float32)
    adam_first = bell_draw(arg_keys[4], (REPLICAS, FF, D), 0.01, 0.06, ((0, 16), (1, 16)), jnp.float32)
    adam_second = jnp.clip(jnp.exp(math.log(0.001) - 6.9077553 * jax.random.uniform(arg_keys[5], (REPLICAS, FF, D), jnp.float32) ** shard_levels(arg_keys[5], (REPLICAS, FF, D), ((0, 16), (1, 16)), -0.2, 0.2)), 9.999999974752427e-07, 0.001)
    base_params = bell_draw(arg_keys[6], (FF, D), D ** -0.5, 0.21875, ((0, 16),), jnp.float32)
    outer_moment = bell_draw(arg_keys[7], (FF, D), 0.01, 0.06, ((0, 16),), jnp.float32)
    return dict(acts=acts, grad_out=grad_out, next_acts=next_acts, inner_params=inner_params, adam_first=adam_first, adam_second=adam_second, base_params=base_params, outer_moment=outer_moment)


def reference(acts, grad_out, next_acts, inner_params, adam_first, adam_second, base_params, outer_moment):
    rows = TOK_DEV * N_FSDP
    corr_one = 1.0 - 0.9 ** INNER_STEP
    corr_two = 1.0 - 0.95 ** INNER_STEP

    def replica(total, index):
        start = (index * rows).astype(jnp.int32)
        inputs = lax.dynamic_slice_in_dim(acts, start, rows, 0)
        cotans = lax.dynamic_slice_in_dim(grad_out, start, rows, 0)
        grad = lax.dot_general(cotans, inputs, (((0,), (0,)), ((), ())), preferred_element_type=jnp.float32) / rows
        moment_one = 0.9 * adam_first[index] + 0.1 * grad
        moment_two = 0.95 * adam_second[index] + 0.05 * grad * grad
        stepped = inner_params[index] - 0.02 * (moment_one / corr_one) / (jnp.sqrt(moment_two / corr_two) + 1e-08)
        return (total + (base_params - stepped), None)
    total, unused = lax.scan(replica, jnp.zeros(base_params.shape, jnp.float32), jnp.arange(N_ISLAND, dtype=jnp.int32))
    mean_delta = total / N_ISLAND
    new_moment = 0.9 * outer_moment + mean_delta
    new_base = base_params - 0.7 * (mean_delta + 0.9 * new_moment)
    fresh = new_base.astype(jnp.bfloat16)
    next_out = lax.dot_general(next_acts, fresh, (((1,), (1,)), ((), ())), preferred_element_type=jnp.float32)
    return (new_base, new_moment, next_out.astype(jnp.bfloat16))
```

```python
import jax
import jax.numpy as jnp
from jax import lax
from jax.experimental import pallas as pl
from jax.experimental.pallas import tpu as pltpu
from jax.sharding import PartitionSpec as P

INNER_STEP = 500
MESH = pl.DeviceIdType.MESH
BF = jnp.bfloat16
F32 = jnp.float32
CHUNKS = ((0, 208, 0, 128), (0, 208, 128, 128))
SPLIT = (False, True)
NB = 4
RB = 208
RELS = (2, 1, 3, 0)
N_SEND = 32


def comm_kernel(
    acts, gout, inner, mom1, mom2, base, omom, nacts,
    w_out, nb_out, nm_out, na_out,
    acts_t, g_v, part,
    s1, r1, s2, r2, s3, r3, s4, r4, s5, r5, r6,
    st_t, base_c, w_v, nb_v, nm_v, na_t, na_v,
    in_sem, gl_sem, gs_sem, gr_sem, bs_sem, br_sem, snd, rcv, out_sem,
):
    isl, fs = lax.axis_index("island"), lax.axis_index("fsdp")
    y, zl = isl // 4, lax.rem(isl, 4)
    zh, x, c = fs // 8, lax.rem(fs // 2, 4), lax.rem(fs, 2)
    z = zh * 4 + zl
    oc, ozh = 1 - c, 1 - zh

    def dev(dx=0, dy=0, dz=0, dc=0):
        nz = lax.rem(z + dz, 8)
        ny, nx, nc = lax.rem(y + dy, 4), lax.rem(x + dx, 4), lax.rem(c + dc, 2)
        return (ny * 4 + lax.rem(nz, 4), ((nz // 4) * 4 + nx) * 2 + nc)

    def remote(src, dst, ss, rs, to):
        return pltpu.make_async_remote_copy(
            src_ref=src, dst_ref=dst, send_sem=ss, recv_sem=rs, device_id=to, device_id_type=MESH
        )

    def col(rel, h, par):
        nx = lax.rem(x + rel, 4)
        return pl.ds(pl.multiple_of(((h * 4 + nx) * 2 + par) * 256, 256), 256)

    load_acts = pltpu.make_async_copy(acts, acts_t.at[0], in_sem.at[0])
    load_acts.start()
    loads = {}
    for n, rel in enumerate(RELS):
        for h in range(2):
            cp = pltpu.make_async_copy(
                gout.at[:, col(rel, h, c)], g_v.at[n, h, pl.ds(0, 512)], gl_sem.at[n * 2 + h]
            )
            cp.start()
            loads[n, h] = cp
    states = []
    for n, ref in enumerate((inner, mom1, mom2, base, omom, nacts)):
        cp = pltpu.make_async_copy(ref, st_t.at[n] if n < 5 else na_t, in_sem.at[1 + n])
        cp.start()
        states.append(cp)

    bar = pltpu.get_barrier_semaphore()
    peers = [dev(dc=1)] + [dev(dx=d) for d in (1, 2, 3)] + [dev(dy=d) for d in (1, 2, 3)]
    peers += [dev(dz=d) for d in range(1, 8)]
    for p in peers:
        pl.semaphore_signal(bar, inc=1, device_id=p, device_id_type=MESH)
    pl.semaphore_wait(bar, len(peers))

    swap_acts = remote(acts, acts_t.at[1], gs_sem.at[8], gr_sem.at[8], dev(dc=1))
    swap_acts.start()
    swaps = {}
    for n, rel in enumerate(RELS):
        for h in range(2):
            cp = remote(
                gout.at[:, col(rel, h, oc)], g_v.at[n, h, pl.ds(512, 512)],
                gs_sem.at[n * 2 + h], gr_sem.at[n * 2 + h], dev(dc=1),
            )
            cp.start()
            swaps[n, h] = cp

    load_acts.wait()
    swap_acts.wait_recv()

    def multiply(n, h, put):
        loads[n, h].wait()
        swaps[n, h].wait_recv()

        def body(b, carry):
            total = jnp.dot(acts_t[0, b], g_v[n, h, :512], preferred_element_type=F32)
            total += jnp.dot(acts_t[1, b], g_v[n, h, 512:], preferred_element_type=F32)
            put(b, total)
            return carry

        lax.fori_loop(0, NB, body, 0)

    def to_bf(ref, h):
        def put(b, value):
            ref[h, b] = value.astype(BF)
        return put

    def to_part(k):
        def put(b, value):
            part[k, b] = value
        return put

    pending = []

    def start(k, slot, src, dst, to):
        cp = remote(src, dst, snd.at[k, slot], rcv.at[k, slot], to)
        cp.start()
        pending.append(cp)
        return cp

    live = {}

    def cut(k):
        r0, rn, l0, ln = CHUNKS[k]
        return pl.ds(r0, rn), pl.ds(l0, ln)

    def t1(k):
        rows, lanes = cut(k)
        for h in range(2):
            live["t1", k, h] = start(
                k, h, s1.at[h, :, rows, lanes], r1.at[h, :, rows, lanes], dev(dx=1 if h == 0 else 3)
            )

    def t2(k):
        rows, lanes = cut(k)
        for h in range(2):
            live["t2", k, h] = start(
                k, 2 + h, s2.at[h, :, rows, lanes], r2.at[h, :, rows, lanes], dev(dx=3 if h == 0 else 1)
            )

    def t3(k):
        rows, lanes = cut(k)
        for h in range(2):
            live["t1", k, h].wait_recv()

            def body(b, carry):
                s3[h, b, rows, lanes] = (
                    part[h, b, rows, lanes] + r1[h, b, rows, lanes].astype(F32)
                ).astype(BF)
                return carry

            lax.fori_loop(0, NB, body, 0)
            live["t3", k, h] = start(
                k, 4 + h, s3.at[h, :, rows, lanes], r3.at[h, :, rows, lanes], dev(dx=1 if h == 0 else 3)
            )

    def t4(k):
        rows, lanes = cut(k)
        for h in range(2):
            live["t2", k, h].wait_recv()
            live["t3", k, h].wait_recv()

        def body(b, carry):
            s4[b, rows, lanes] = (
                part[2 + ozh, b, rows, lanes]
                + r2[ozh, b, rows, lanes].astype(F32)
                + r3[ozh, b, rows, lanes].astype(F32)
            ).astype(BF)
            return carry

        lax.fori_loop(0, NB, body, 0)
        live["t4", k] = start(k, 6, s4.at[:, rows, lanes], r4.at[:, rows, lanes], dev(dz=4))

    corr_one = 1.0 - 0.9**INNER_STEP
    corr_two = 1.0 - 0.95**INNER_STEP

    def t5(k):
        rows, lanes = cut(k)
        live["t4", k].wait_recv()

        def body(b, carry):
            grad = (
                part[2 + zh, b, rows, lanes]
                + r2[zh, b, rows, lanes].astype(F32)
                + r3[zh, b, rows, lanes].astype(F32)
                + r4[b, rows, lanes].astype(F32)
            ) * (1.0 / 8192.0)
            one = 0.9 * st_t[1, b, rows, lanes] + 0.1 * grad
            two = 0.95 * st_t[2, b, rows, lanes] + 0.05 * grad * grad
            step = (one * (0.02 / corr_one)) / (jnp.sqrt(two * (1.0 / corr_two)) + 1e-08)
            s5[b, rows, lanes] = st_t[3, b, rows, lanes] - (st_t[0, b, rows, lanes] - step)
            return carry

        lax.fori_loop(0, NB, body, 0)
        for d in (1, 2, 3):
            live["t5", k, d] = start(
                k, 6 + d, s5.at[lax.rem(y + d, 4), rows, lanes], r5.at[d - 1, rows, lanes], dev(dy=d)
            )

    def t6(k):
        rows, lanes = cut(k)
        for d in (1, 2, 3):
            live["t5", k, d].wait_recv()
        total = s5[y, rows, lanes]
        for d in range(3):
            total += r5[d, rows, lanes]
        r6[z, rows, lanes] = total.astype(BF)
        for d in range(1, 8):
            live["t6", k, d] = start(
                k, 9 + d, r6.at[z, rows, lanes], r6.at[z, rows, lanes], dev(dz=d)
            )

    def t7(k):
        rows, lanes = cut(k)
        for d in range(1, 8):
            live["t6", k, d].wait_recv()
        if k == 0:
            live["base"].wait_recv()

        def mean(h):
            total = r6[4 * h, rows, lanes].astype(F32)
            for m in range(1, 4):
                total += r6[4 * h + m, rows, lanes].astype(F32)
            return total * (1.0 / 16.0)

        for h in range(2):
            w_v[c, h, x, y, rows, lanes] = (base_c[h, rows, lanes] - 1.33 * mean(h)).astype(BF)
        own = mean(zh)
        nb_v[rows, lanes] = base_c[zh, rows, lanes] - 1.33 * own
        nm_v[rows, lanes] = 0.9 * st_t[4, y, rows, lanes] + own
        if SPLIT[k]:
            for d in (1, 2, 3):
                ref = w_v.at[c, 0, x, y, rows, lanes]
                live["t7", k, 0, d] = start(k, 16 + d, ref, ref, dev(dx=d))
                ref = w_v.at[c, 1, x, y, rows, lanes]
                live["t7", k, 1, d] = start(k, 19 + d, ref, ref, dev(dy=d))
        else:
            for d in (1, 2, 3):
                ref = w_v.at[c, :, x, y, rows, lanes]
                live["t7", k, 0, d] = start(k, 16 + d, ref, ref, dev(dx=d))

    def to_core(k, slot, ref):
        live["core", k, slot] = start(k, slot, ref, ref, dev(dc=1))

    def t8(k):
        rows, lanes = cut(k)
        if SPLIT[k]:
            for h in range(2):
                for d in (1, 2, 3):
                    live["t7", k, h, d].wait_recv()
                ref = w_v.at[c, 0, :, y, rows, lanes] if h == 0 else w_v.at[c, 1, x, :, rows, lanes]
                for d in (1, 2, 3):
                    to = dev(dy=d) if h == 0 else dev(dx=d)
                    live["t8", k, h, d] = start(k, 22 + 3 * h + d, ref, ref, to)
                to_core(k, 29 + h, ref)
        else:
            for d in (1, 2, 3):
                live["t7", k, 0, d].wait_recv()
            ref = w_v.at[c, :, :, y, rows, lanes]
            for d in (1, 2, 3):
                live["t8", k, 0, d] = start(k, 22 + d, ref, ref, dev(dy=d))
            to_core(k, 29, ref)

    def t9(k):
        rows, lanes = cut(k)
        for d in (1, 3, 2):
            if SPLIT[k]:
                for h in range(2):
                    live["t8", k, h, d].wait_recv()
                    ref = (
                        w_v.at[c, 0, :, lax.rem(y + 4 - d, 4), rows, lanes]
                        if h == 0
                        else w_v.at[c, 1, lax.rem(x + 4 - d, 4), :, rows, lanes]
                    )
                    to_core(k, 30 + h * 3 + d, ref)
            else:
                live["t8", k, 0, d].wait_recv()
                to_core(k, 30 + d, w_v.at[c, :, :, lax.rem(y + 4 - d, 4), rows, lanes])

    outs = []

    def t10(k):
        rows, lanes = cut(k)
        for key, cp in live.items():
            if key[0] == "core" and key[1] == k:
                cp.wait_recv()
        for p in range(2):
            for h in range(2):
                cp = pltpu.make_async_copy(
                    w_v.at[p, h, :, :, rows, lanes], w_out.at[p, h, :, :, rows, lanes],
                    out_sem.at[k * 4 + p * 2 + h],
                )
                cp.start()
                outs.append(cp)

    def stage_mul():
        multiply(0, 0, to_bf(s1, 0))
        multiply(0, 1, to_bf(s1, 1))
        t1(0)
        multiply(1, 1, to_bf(s2, 1))
        multiply(2, 0, to_bf(s2, 0))
        t2(0)
        t1(1)
        multiply(1, 0, to_part(0))
        multiply(2, 1, to_part(1))
        multiply(3, 0, to_part(2))
        multiply(3, 1, to_part(3))

    def stage_base():
        states[3].wait()
        states[4].wait()
        base_c[zh] = st_t[3, y] - 0.567 * st_t[4, y]
        live["base"] = remote(base_c.at[zh], base_c.at[zh], bs_sem, br_sem, dev(dz=4))
        live["base"].start()
        pending.append(live["base"])

    def stage_rest():
        for n in (0, 1, 2, 5):
            states[n].wait()
        na_v[...] = na_t[...].T
        cp = pltpu.make_async_copy(na_v, na_out, out_sem.at[4 * len(CHUNKS) + 2])
        cp.start()
        outs.append(cp)

    steps = [
        (stage_mul,), (stage_base,), (t3, 0), (t2, 1), (stage_rest,), (t4, 0), (t3, 1), (t5, 0), (t4, 1),
        (t6, 0), (t7, 0), (t5, 1), (t8, 0), (t6, 1), (t9, 0), (t7, 1), (t10, 0), (t8, 1), (t9, 1), (t10, 1),
    ]
    for step in steps:
        step[0](*step[1:])
    for n, (src, dst) in enumerate(((nb_v, nb_out), (nm_v, nm_out))):
        cp = pltpu.make_async_copy(src, dst, out_sem.at[4 * len(CHUNKS) + n])
        cp.start()
        outs.append(cp)
    swap_acts.wait_send()
    for cp in swaps.values():
        cp.wait_send()
    for cp in pending:
        cp.wait_send()
    for cp in outs:
        cp.wait()


def project_kernel(a_ref, w_ref, nb_ref, nm_ref, o_ref, nbo_ref, nmo_ref):
    o_ref[...] = jnp.dot(
        a_ref[...], w_ref[...].reshape(NB * RB, 256), preferred_element_type=F32
    ).astype(BF)
    zl = lax.rem(lax.axis_index("island"), 4)

    @pl.when(pl.program_id(0) == 0)
    def _():
        for k in range(4):
            @pl.when(zl == k)
            def _():
                nbo_ref[...] = nb_ref[pl.ds(52 * k, 52), :]
                nmo_ref[...] = nm_ref[pl.ds(52 * k, 52), :]


def per_device(
    acts, grad_out, next_acts, inner_params, adam_first, adam_second, base_params, outer_moment
):
    n = len(CHUNKS)
    dma, vm = pltpu.SemaphoreType.DMA, pltpu.VMEM
    hbm = pl.BlockSpec(memory_space=pl.ANY)
    block = (NB, RB, 256)
    acts_tr = acts.T.reshape(NB, RB, 512)
    states = [a[0].T.reshape(block) for a in (inner_params, adam_first, adam_second)]
    states += [a.T.reshape(block) for a in (base_params, outer_moment)]
    w, nb, nm, na = pl.pallas_call(
        comm_kernel,
        out_shape=(
            jax.ShapeDtypeStruct((2, 2, 4) + block, BF),
            jax.ShapeDtypeStruct((RB, 256), F32),
            jax.ShapeDtypeStruct((RB, 256), F32),
            jax.ShapeDtypeStruct((512, 832), BF),
        ),
        in_specs=[hbm] * 8,
        out_specs=(hbm,) * 4,
        scratch_shapes=[
            vm((2, NB, RB, 512), BF), vm((4, 2, 1024, 256), BF),
            vm((4,) + block, F32),
            vm((2,) + block, BF), vm((2,) + block, BF), vm((2,) + block, BF), vm((2,) + block, BF),
            vm((2,) + block, BF), vm((2,) + block, BF), vm(block, BF), vm(block, BF), vm(block, F32),
            vm((3, RB, 256), F32), vm((8, RB, 256), BF),
            vm((5,) + block, F32), vm((2, RB, 256), F32),
            vm((2, 2, 4) + block, BF), vm((RB, 256), F32), vm((RB, 256), F32),
            vm((832, 512), BF), vm((512, 832), BF),
            dma((7,)), dma((8,)), dma((9,)), dma((9,)), dma, dma,
            dma((n, 40)), dma((n, 40)), dma((4 * n + 3,)),
        ],
        compiler_params=pltpu.CompilerParams(
            collective_id=0, has_side_effects=True, vmem_limit_bytes=60 * 2**20
        ),
        name="outer_round",
    )(acts_tr, grad_out, *states, next_acts.T)
    whole = pl.BlockSpec((RB, 256), lambda i: (0, 0))
    small = pl.BlockSpec((52, 256), lambda i: (0, 0))
    next_out, base_out, moment_out = pl.pallas_call(
        project_kernel,
        grid=(16,),
        out_shape=(
            jax.ShapeDtypeStruct((512, 4096), BF),
            jax.ShapeDtypeStruct((52, 256), F32),
            jax.ShapeDtypeStruct((52, 256), F32),
        ),
        in_specs=[
            pl.BlockSpec((512, 832), lambda i: (0, 0)),
            pl.BlockSpec((None, None, None) + block, lambda i: (i % 2, i // 8, (i // 2) % 4, 0, 0, 0)),
            whole,
            whole,
        ],
        out_specs=(pl.BlockSpec((512, 256), lambda i: (0, i)), small, small),
        compiler_params=pltpu.CompilerParams(vmem_limit_bytes=60 * 2**20),
        name="project",
    )(na, w, nb, nm)
    return base_out.T, moment_out.T, next_out


def solution(mesh):
    in_specs = (
        P(("island", "fsdp"), None),
        P(("island", "fsdp"), None),
        P(("island", "fsdp"), None),
        P("island", "fsdp", None),
        P("island", "fsdp", None),
        P("island", "fsdp", None),
        P("fsdp", None),
        P("fsdp", None),
    )
    out_specs = (P("fsdp", "island"), P("fsdp", "island"), P(("island", "fsdp"), None))
    return jax.shard_map(
        per_device, mesh=mesh, in_specs=in_specs, out_specs=out_specs, check_vma=False
    )
```

```python
import jax
import jax.numpy as jnp
from jax import lax
from jax.experimental import pallas as pl
from jax.experimental.pallas import tpu as pltpu
from jax.sharding import PartitionSpec as P

INNER_STEP = 500
MESH = pl.DeviceIdType.MESH
BF = jnp.bfloat16
F32 = jnp.float32
CHUNKS = (
    (0, 48, 0, 128), (48, 64, 0, 128), (112, 96, 0, 128), (0, 96, 128, 128), (96, 64, 128, 128), (160, 48, 128, 128)
)
FIRST = (32, 32, 48, 48, 32, 32)
WIDE = (4, 5)
DIRECT = (10, 9, 11, 6, 14, 2, 8, 5, 7, 13, 15, 1, 3, 4, 12)
WIDE_ROWS, WIDE_LANES = pl.ds(96, 112), pl.ds(128, 128)
NB = 4
RB = 208
RELS = (2, 1, 3, 0)


def comm_kernel(
    acts, gout, inner, mom1, mom2, base, omom, nacts,
    w_v, nb_v, nm_v, na_v, half_v,
    acts_t, g_v, xs, xr, part,
    s1, r1, s2, r2, s3, r3, s4, r4, s5, r5, r6,
    st_t, na_t, base_c,
    in_sem, gl_sem, xs_sem, xr_sem, bs_sem, br_sem, snd, rcv,
):
    isl, fs = lax.axis_index("island"), lax.axis_index("fsdp")
    y, zl = isl // 4, lax.rem(isl, 4)
    zh, x, c = fs // 8, lax.rem(fs // 2, 4), lax.rem(fs, 2)
    oc, ozh = 1 - c, 1 - zh

    def dev(dx=0, dy=0, dl=0, dh=0, dc=0):
        ny, nl = lax.rem(y + dy, 4), lax.rem(zl + dl, 4)
        nh, nx, nc = lax.rem(zh + dh, 2), lax.rem(x + dx, 4), lax.rem(c + dc, 2)
        return (ny * 4 + nl, (nh * 4 + nx) * 2 + nc)

    def remote(src, dst, ss, rs, to):
        return pltpu.make_async_remote_copy(
            src_ref=src, dst_ref=dst, send_sem=ss, recv_sem=rs, device_id=to, device_id_type=MESH
        )

    def col(rel, h, par):
        nx = lax.rem(x + rel, 4)
        return pl.ds(pl.multiple_of(((h * 4 + nx) * 2 + par) * 256, 256), 256)

    loads = {}

    def load(n):
        for side, par in enumerate((oc, c)):
            for h in range(2):
                loads[n, side, h] = pltpu.make_async_copy(
                    gout.at[:, col(RELS[n], h, par)], g_v.at[n, side, h], gl_sem.at[n, side, h]
                )
                loads[n, side, h].start()

    load_acts = pltpu.make_async_copy(acts, acts_t, in_sem.at[0])
    load_acts.start()
    load(0)

    bar = pltpu.get_barrier_semaphore()
    peers = [dev(dc=1)] + [dev(dl=d, dh=1) for d in range(4)]
    peers += [dev(dx=d % 4, dy=d // 4) for d in range(1, 16)] + [dev(dl=d) for d in (1, 2, 3)]
    for p in peers:
        pl.semaphore_signal(bar, inc=1, device_id=p, device_id_type=MESH)
    load(1)

    states = []

    def load_states():
        for n, ref in enumerate((inner, mom1, mom2, base, omom, nacts)):
            cp = pltpu.make_async_copy(ref, st_t.at[n] if n < 5 else na_t, in_sem.at[1 + n])
            cp.start()
            states.append(cp)

    swaps = {}

    def give_mul(n, h):
        loads[n, 0, h].wait()
        value = jnp.dot(acts_t[...].reshape(NB * RB, 512), g_v[n, 0, h], preferred_element_type=F32)
        xs[n, h] = value.astype(BF).reshape(NB, RB, 256)

    def give_send(n, h, q=None):
        lanes = pl.ds(0, 256) if q is None else pl.ds(q * 128, 128)
        m = q or 0
        swaps[n, h, q] = remote(
            xs.at[n, h, :, :, lanes], xr.at[n, h, :, :, lanes], xs_sem.at[n, h, m], xr_sem.at[n, h, m], dev(dc=1)
        )
        swaps[n, h, q].start()

    def keep(n, h, ref, q=None):
        swaps[n, h, q].wait_recv()
        lanes = pl.ds(0, 256) if q is None else pl.ds(q * 128, 128)
        if (n, h) not in kept:
            loads[n, 1, h].wait()
            kept.add((n, h))

        value = jnp.dot(
            acts_t[...].reshape(NB * RB, 512), g_v[n, 1, h, :, lanes], preferred_element_type=F32
        )
        value = value.reshape(NB, RB, value.shape[1]) + xr[n, h, :, :, lanes].astype(F32)
        ref[:, :, lanes] = value.astype(ref.dtype)

    kept = set()
    pending = []

    def start(k, slot, src, dst, to):
        cp = remote(src, dst, snd.at[k, slot], rcv.at[k, slot], to)
        cp.start()
        pending.append(cp)
        return cp

    live = {}

    def cut(k):
        r0, rn, l0, ln = CHUNKS[k]
        return pl.ds(r0, rn), pl.ds(l0, ln)

    def t1(k, halves=(0, 1)):
        rows, lanes = cut(k)
        for h in halves:
            live["t1", k, h] = start(
                k, h, s1.at[h, :, rows, lanes], r1.at[h, :, rows, lanes], dev(dx=1 if h == 0 else 3)
            )

    def t2(k):
        rows, lanes = cut(k)
        for h in range(2):
            live["t2", k, h] = start(
                k, 2 + h, s2.at[h, :, rows, lanes], r2.at[h, :, rows, lanes], dev(dx=3 if h == 0 else 1)
            )

    def t3(k):
        rows, lanes = cut(k)
        for h in range(2):
            live["t1", k, h].wait_recv()

            def body(b, carry):
                s3[h, b, rows, lanes] = (
                    part[h, b, rows, lanes] + r1[h, b, rows, lanes].astype(F32)
                ).astype(BF)
                return carry

            lax.fori_loop(0, NB, body, 0)
            live["t3", k, h] = start(
                k, 4 + h, s3.at[h, :, rows, lanes], r3.at[h, :, rows, lanes], dev(dx=1 if h == 0 else 3)
            )

    def t4(k):
        rows, lanes = cut(k)
        for h in range(2):
            live["t2", k, h].wait_recv()
            live["t3", k, h].wait_recv()

        def body(b, carry):
            s4[b, rows, lanes] = (
                part[2 + ozh, b, rows, lanes]
                + r2[ozh, b, rows, lanes].astype(F32)
                + r3[ozh, b, rows, lanes].astype(F32)
            ).astype(BF)
            return carry

        lax.fori_loop(0, NB, body, 0)
        live["t4", k] = start(k, 6, s4.at[:, rows, lanes], r4.at[:, rows, lanes], dev(dh=1))

    corr_one = 1.0 - 0.9**INNER_STEP
    corr_two = 1.0 - 0.95**INNER_STEP

    def t5(k):
        rows, lanes = cut(k)
        live["t4", k].wait_recv()

        def body(b, carry):
            grad = (
                part[2 + zh, b, rows, lanes]
                + r2[zh, b, rows, lanes].astype(F32)
                + r3[zh, b, rows, lanes].astype(F32)
                + r4[b, rows, lanes].astype(F32)
            ) * (1.0 / 8192.0)
            one = 0.9 * st_t[1, b, rows, lanes] + 0.1 * grad
            two = 0.95 * st_t[2, b, rows, lanes] + 0.05 * grad * grad
            step = (one * (0.02 / corr_one)) / (jnp.sqrt(two * (1.0 / corr_two)) + 1e-08)
            s5[b, rows, lanes] = st_t[3, b, rows, lanes] - (st_t[0, b, rows, lanes] - step)
            return carry

        lax.fori_loop(0, NB, body, 0)
        for d in (1, 2, 3):
            live["t5", k, d] = start(
                k, 6 + d, s5.at[lax.rem(y + d, 4), rows, lanes], r5.at[d - 1, rows, lanes], dev(dy=d)
            )

    def t6(k):
        rows, lanes = cut(k)
        for d in (1, 2, 3):
            live["t5", k, d].wait_recv()
        total = s5[y, rows, lanes]
        for d in range(3):
            total += r5[d, rows, lanes]
        slot = zh * 4 + zl
        r6[slot, rows, lanes] = total.astype(BF)
        ref = r6.at[slot, rows, lanes]
        for d in (1, 2, 3):
            live["t6", k, d] = start(k, 9 + d, ref, ref, dev(dl=d))
        if k in WIDE:
            for d in range(4):
                live["t6", k, 4 + d] = start(k, 40 + d, ref, ref, dev(dl=d, dh=1))

    def parts_of(k):
        r0, rn, l0, ln = CHUNKS[k]
        return (pl.ds(r0, FIRST[k]), pl.ds(r0 + FIRST[k], rn - FIRST[k])), pl.ds(l0, ln)

    def gather_one(k, other):
        (first, second), lanes = parts_of(k)
        h = ozh if other else zh
        for d in (1, 2, 3):
            ref = w_v.at[c, h, x, y, first, lanes]
            live["mid", k, other, 0, d] = start(k, 13 + 6 * other + d, ref, ref, dev(dx=d))
            ref = w_v.at[c, h, x, y, second, lanes]
            live["mid", k, other, 1, d] = start(k, 16 + 6 * other + d, ref, ref, dev(dy=d))

    def t7(k):
        rows, lanes = cut(k)
        for d in (1, 2, 3):
            live["t6", k, d].wait_recv()
        if k in WIDE:
            for d in range(4):
                live["t6", k, 4 + d].wait_recv()

        def average(h):
            total = r6[h * 4, rows, lanes].astype(F32)
            for m in range(1, 4):
                total += r6[h * 4 + m, rows, lanes].astype(F32)
            return total * (1.0 / 16.0)

        mean = average(zh)
        moment = 0.9 * st_t[4, y, rows, lanes] + mean
        fresh = st_t[3, y, rows, lanes] - 0.7 * (mean + 0.9 * moment)
        w_v[c, zh, x, y, rows, lanes] = fresh.astype(BF)
        if k in WIDE:
            if "base" in live:
                live.pop("base").wait_recv()
            w_v[c, ozh, x, y, rows, lanes] = (base_c[1, rows, lanes] - 1.33 * average(ozh)).astype(BF)
            ref = w_v.at[c, :, x, y, rows, lanes]
            for d in DIRECT:
                live["all", k, d] = start(k, 13 + d, ref, ref, dev(dx=d % 4, dy=d // 4))
        else:
            ref = w_v.at[c, zh, x, y, rows, lanes]
            live["t7", k] = start(k, 13, ref, ref, dev(dh=1))
            gather_one(k, 0)
        nb_v[rows, lanes] = fresh
        nm_v[rows, lanes] = moment

    def t7b(k):
        live["t7", k].wait_recv()
        gather_one(k, 1)

    def gather_two(k, other):
        (first, second), lanes = parts_of(k)
        h = ozh if other else zh
        for p in range(2):
            for d in (1, 2, 3):
                live["mid", k, other, p, d].wait_recv()
            ref = w_v.at[c, h, :, y, first, lanes] if p == 0 else w_v.at[c, h, x, :, second, lanes]
            for d in (1, 2, 3):
                live["end", k, other, p, d] = start(
                    k, 25 + 6 * other + 3 * p + d, ref, ref, dev(dy=d) if p == 0 else dev(dx=d)
                )

    def gather_three(k, other):
        rows, lanes = cut(k)
        for p in range(2):
            for d in (1, 2, 3):
                live["end", k, other, p, d].wait_recv()
        ref = w_v.at[c, ozh if other else zh, :, :, rows, lanes]
        live["core", k, other] = start(k, 38 + other, ref, ref, dev(dc=1))

    def gather_all(k):
        rows, lanes = cut(k)
        for d in DIRECT:
            live["all", k, d].wait_recv()
        ref = w_v.at[c, :, :, :, rows, lanes]
        live["core", k, 0] = start(k, 38, ref, ref, dev(dc=1))

    def t10(k):
        live["core", k, 0].wait_recv()
        if k not in WIDE:
            live["core", k, 1].wait_recv()

    def stage_mul():
        load_acts.wait()
        give_mul(0, 0)
        give_mul(0, 1)
        load(2)
        load(3)
        pl.semaphore_wait(bar, len(peers))
        give_send(0, 0, 0)
        give_send(0, 1, 0)
        load_states()
        give_mul(1, 1)
        give_mul(2, 0)
        keep(0, 0, s1.at[0], 0)
        t1(0, (0,))
        t1(1, (0,))
        keep(0, 1, s1.at[1], 0)
        t1(0, (1,))
        t1(1, (1,))
        give_send(0, 0, 1)
        give_send(0, 1, 1)
        give_send(1, 1)
        give_send(2, 0)
        give_mul(1, 0)
        give_mul(2, 1)
        keep(1, 1, s2.at[1])
        keep(2, 0, s2.at[0])
        t2(0)
        give_send(1, 0)
        give_send(2, 1)
        keep(0, 0, s1.at[0], 1)
        keep(0, 1, s1.at[1], 1)
        for n, h in ((3, 0), (3, 1)):
            give_mul(n, h)
            give_send(n, h)
        for m, (n, h) in enumerate(((1, 0), (2, 1), (3, 0), (3, 1))):
            keep(n, h, part.at[m])

    def stage_rest():
        for cp in states:
            cp.wait()
        mine = st_t[3, y, WIDE_ROWS, WIDE_LANES] - 0.567 * st_t[4, y, WIDE_ROWS, WIDE_LANES]
        base_c[0, WIDE_ROWS, WIDE_LANES] = mine
        live["base"] = remote(
            base_c.at[0, WIDE_ROWS, WIDE_LANES], base_c.at[1, WIDE_ROWS, WIDE_LANES], bs_sem, br_sem, dev(dh=1)
        )
        live["base"].start()
        pending.append(live["base"])
        na_v[...] = na_t[...].T

    def product(p, hh):
        for xx in range(0, 4, 2):
            pair = jnp.concatenate(
                [w_v[p, hh, xx + m, :, :, :128].reshape(NB * RB, 128) for m in range(2)], axis=1
            )
            half_v[p, hh, xx // 2] = jnp.dot(na_v[...], pair, preferred_element_type=F32).astype(BF)

    done = []

    def drain(keep_last):
        n = len(pending) - keep_last
        for cp in pending[len(done) : n]:
            cp.wait_send()
            done.append(cp)

    steps = [
        (stage_mul,), (t2, 1), (t3, 0), (t3, 1), (t1, 2), (t2, 2), (t4, 0), (t4, 1), (t3, 2), (t1, 3),
        (stage_rest,), (t5, 0), (t2, 3), (t4, 2), (t5, 1), (t3, 3), (t6, 0), (t1, 5), (t2, 5), (t2, 4), (t6, 1),
        (t4, 3), (t3, 5), (t1, 4), (t5, 2), (t7, 0), (drain, 40), (t4, 5), (t3, 4), (t7, 1), (t6, 2), (t5, 3),
        (t7b, 0), (t4, 4), (gather_two, 0, 0), (t5, 5), (t7b, 1), (gather_two, 1, 0), (t6, 3), (t7, 2),
        (drain, 40), (gather_two, 0, 1), (t6, 5), (gather_three, 0, 0), (t5, 4), (gather_two, 1, 1),
        (gather_three, 1, 0), (t7, 3), (gather_two, 2, 0), (t6, 4), (t7b, 2), (gather_two, 3, 0), (t7, 5),
        (drain, 60), (gather_three, 1, 1), (t7b, 3), (gather_two, 2, 1), (t7, 4), (drain, 60),
        (gather_three, 0, 1), (gather_all, 5), (gather_two, 3, 1), (gather_three, 2, 1), (gather_three, 2, 0),
        (t10, 1), (t10, 0), (gather_three, 3, 0), (gather_all, 4), (t10, 5), (t10, 2), (gather_three, 3, 1),
        (product, 0, 1), (product, 1, 0), (product, 0, 0), (t10, 4), (product, 1, 1), (t10, 3),
    ]
    for step in steps:
        step[0](*step[1:])
    for cp in swaps.values():
        cp.wait_send()
    drain(0)


def project_kernel(a_ref, w_ref, nb_ref, nm_ref, half_ref, o_ref, nbo_ref, nmo_ref):
    step = pl.program_id(0)
    hh, pr = step // 2, lax.rem(step, 2)
    for p in range(2):
        pair = jnp.concatenate(
            [w_ref[p, hh, pr * 2 + m, :, :, 128:].reshape(NB * RB, 128) for m in range(2)], axis=1
        )
        out = jnp.dot(a_ref[...], pair, preferred_element_type=F32).astype(BF)
        for m in range(2):
            lo = (m * 2 + p) * 256
            o_ref[:, lo : lo + 128] = half_ref[p, hh, pr, :, m * 128 : (m + 1) * 128]
            o_ref[:, lo + 128 : lo + 256] = out[:, m * 128 : (m + 1) * 128]
    zl = lax.rem(lax.axis_index("island"), 4)

    @pl.when(step == 0)
    def _():
        for k in range(4):
            @pl.when(zl == k)
            def _():
                nbo_ref[...] = nb_ref[pl.ds(52 * k, 52), :]
                nmo_ref[...] = nm_ref[pl.ds(52 * k, 52), :]


def per_device(
    acts, grad_out, next_acts, inner_params, adam_first, adam_second, base_params, outer_moment
):
    n = len(CHUNKS)
    dma, vm = pltpu.SemaphoreType.DMA, pltpu.VMEM
    hbm = pl.BlockSpec(memory_space=pl.ANY)
    block = (NB, RB, 256)
    acts_tr = acts.T.reshape(NB, RB, 512)
    states = [a[0].T.reshape(block) for a in (inner_params, adam_first, adam_second)]
    states += [a.T.reshape(block) for a in (base_params, outer_moment)]
    w, nb, nm, na, half = pl.pallas_call(
        comm_kernel,
        out_shape=(
            vm((2, 2, 4) + block, BF), vm((RB, 256), F32), vm((RB, 256), F32), vm((512, 832), BF),
            vm((2, 2, 2, 512, 256), BF),
        ),
        in_specs=[hbm] * 8,
        out_specs=(pl.BlockSpec(memory_space=vm),) * 5,
        scratch_shapes=[
            vm((NB, RB, 512), BF), vm((4, 2, 2, 512, 256), BF), vm((4, 2) + block, BF), vm((4, 2) + block, BF),
            vm((4,) + block, F32),
            vm((2,) + block, BF), vm((2,) + block, BF), vm((2,) + block, BF), vm((2,) + block, BF),
            vm((2,) + block, BF), vm((2,) + block, BF), vm(block, BF), vm(block, BF), vm(block, F32),
            vm((3, RB, 256), F32), vm((8, RB, 256), BF),
            vm((5,) + block, F32), vm((832, 512), BF), vm((2, RB, 256), F32),
            dma((7,)), dma((4, 2, 2)), dma((4, 2, 2)), dma((4, 2, 2)), dma, dma, dma((n, 44)), dma((n, 44)),
        ],
        compiler_params=pltpu.CompilerParams(
            collective_id=0, has_side_effects=True, vmem_limit_bytes=48 * 2**20
        ),
        name="outer_round",
    )(acts_tr, grad_out, *states, next_acts.T)
    whole = pl.BlockSpec(memory_space=vm)
    small = pl.BlockSpec((52, 256), lambda i: (0, 0))
    next_out, base_out, moment_out = pl.pallas_call(
        project_kernel,
        grid=(4,),
        out_shape=(
            jax.ShapeDtypeStruct((512, 4096), BF),
            jax.ShapeDtypeStruct((52, 256), F32),
            jax.ShapeDtypeStruct((52, 256), F32),
        ),
        in_specs=[
            whole,
            whole,
            whole,
            whole,
            whole,
        ],
        out_specs=(pl.BlockSpec((512, 1024), lambda i: (0, i)), small, small),
        compiler_params=pltpu.CompilerParams(vmem_limit_bytes=24 * 2**20),
        name="project",
    )(na, w, nb, nm, half)
    return base_out.T, moment_out.T, next_out


def solution(mesh):
    in_specs = (
        P(("island", "fsdp"), None),
        P(("island", "fsdp"), None),
        P(("island", "fsdp"), None),
        P("island", "fsdp", None),
        P("island", "fsdp", None),
        P("island", "fsdp", None),
        P("fsdp", None),
        P("fsdp", None),
    )
    out_specs = (P("fsdp", "island"), P("fsdp", "island"), P(("island", "fsdp"), None))
    return jax.shard_map(
        per_device, mesh=mesh, in_specs=in_specs, out_specs=out_specs, check_vma=False
    )
```

```python
import jax
import jax.numpy as jnp
from jax import lax
from jax.experimental import pallas as pl
from jax.experimental.pallas import tpu as pltpu
from jax.sharding import PartitionSpec as P

INNER_STEP = 500
MESH = pl.DeviceIdType.MESH
BF = jnp.bfloat16
F32 = jnp.float32
CHUNKS = (
    (0, 48, 0, 128), (48, 64, 0, 128), (112, 96, 0, 128), (0, 64, 128, 128), (64, 64, 128, 128), (128, 48, 128, 128), (176, 32, 128, 128)
)
FIRST = (32, 32, 48, 32, 32, 32, 16)
WIDE = (5, 6)
DIRECT = (10, 9, 11, 6, 14, 2, 8, 5, 7, 13, 15, 1, 3, 4, 12)
WIDE_ROWS, WIDE_LANES = pl.ds(128, 80), pl.ds(128, 128)
NB = 4
RB = 208
RELS = (2, 1, 3, 0)


def comm_kernel(
    acts, gout, inner, mom1, mom2, base, omom, nacts,
    w_v, nb_v, nm_v, na_v, half_v,
    acts_t, g_v, xs, xr, part,
    s1, r1, s2, r2, s3, r3, s4, r4, s5, r5, r6,
    st_t, na_t, base_c,
    in_sem, gl_sem, xs_sem, xr_sem, bs_sem, br_sem, snd, rcv,
):
    isl, fs = lax.axis_index("island"), lax.axis_index("fsdp")
    y, zl = isl // 4, lax.rem(isl, 4)
    zh, x, c = fs // 8, lax.rem(fs // 2, 4), lax.rem(fs, 2)
    oc, ozh = 1 - c, 1 - zh

    def dev(dx=0, dy=0, dl=0, dh=0, dc=0):
        ny, nl = lax.rem(y + dy, 4), lax.rem(zl + dl, 4)
        nh, nx, nc = lax.rem(zh + dh, 2), lax.rem(x + dx, 4), lax.rem(c + dc, 2)
        return (ny * 4 + nl, (nh * 4 + nx) * 2 + nc)

    def remote(src, dst, ss, rs, to):
        return pltpu.make_async_remote_copy(
            src_ref=src, dst_ref=dst, send_sem=ss, recv_sem=rs, device_id=to, device_id_type=MESH
        )

    def col(rel, h, par):
        nx = lax.rem(x + rel, 4)
        return pl.ds(pl.multiple_of(((h * 4 + nx) * 2 + par) * 256, 256), 256)

    loads = {}

    def load(n):
        for side, par in enumerate((oc, c)):
            for h in range(2):
                loads[n, side, h] = pltpu.make_async_copy(
                    gout.at[:, col(RELS[n], h, par)], g_v.at[n, side, h], gl_sem.at[n, side, h]
                )
                loads[n, side, h].start()

    load_acts = pltpu.make_async_copy(acts, acts_t, in_sem.at[0])
    load_acts.start()
    load(0)

    bar = pltpu.get_barrier_semaphore()
    peers = [dev(dc=1)] + [dev(dl=d, dh=1) for d in range(4)]
    peers += [dev(dx=d % 4, dy=d // 4) for d in range(1, 16)] + [dev(dl=d) for d in (1, 2, 3)]
    for p in peers:
        pl.semaphore_signal(bar, inc=1, device_id=p, device_id_type=MESH)
    load(1)

    states = []

    def load_states():
        for n, ref in enumerate((inner, mom1, mom2, base, omom, nacts)):
            cp = pltpu.make_async_copy(ref, st_t.at[n] if n < 5 else na_t, in_sem.at[1 + n])
            cp.start()
            states.append(cp)

    swaps = {}

    def give_mul(n, h):
        loads[n, 0, h].wait()
        value = jnp.dot(acts_t[...].reshape(NB * RB, 512), g_v[n, 0, h], preferred_element_type=F32)
        xs[n, h] = value.astype(BF).reshape(NB, RB, 256)

    def give_send(n, h, q=None):
        lanes = pl.ds(0, 256) if q is None else pl.ds(q * 128, 128)
        m = q or 0
        swaps[n, h, q] = remote(
            xs.at[n, h, :, :, lanes], xr.at[n, h, :, :, lanes], xs_sem.at[n, h, m], xr_sem.at[n, h, m], dev(dc=1)
        )
        swaps[n, h, q].start()

    def keep(n, h, ref, q=None):
        swaps[n, h, q].wait_recv()
        lanes = pl.ds(0, 256) if q is None else pl.ds(q * 128, 128)
        if (n, h) not in kept:
            loads[n, 1, h].wait()
            kept.add((n, h))

        value = jnp.dot(
            acts_t[...].reshape(NB * RB, 512), g_v[n, 1, h, :, lanes], preferred_element_type=F32
        )
        value = value.reshape(NB, RB, value.shape[1]) + xr[n, h, :, :, lanes].astype(F32)
        ref[:, :, lanes] = value.astype(ref.dtype)

    kept = set()
    pending = []

    def start(k, slot, src, dst, to):
        cp = remote(src, dst, snd.at[k, slot], rcv.at[k, slot], to)
        cp.start()
        pending.append(cp)
        return cp

    live = {}

    def cut(k):
        r0, rn, l0, ln = CHUNKS[k]
        return pl.ds(r0, rn), pl.ds(l0, ln)

    def t1(k, halves=(0, 1)):
        rows, lanes = cut(k)
        for h in halves:
            live["t1", k, h] = start(
                k, h, s1.at[h, :, rows, lanes], r1.at[h, :, rows, lanes], dev(dx=1 if h == 0 else 3)
            )

    def t2(k):
        rows, lanes = cut(k)
        for h in range(2):
            live["t2", k, h] = start(
                k, 2 + h, s2.at[h, :, rows, lanes], r2.at[h, :, rows, lanes], dev(dx=3 if h == 0 else 1)
            )

    def t3(k):
        rows, lanes = cut(k)
        for h in range(2):
            live["t1", k, h].wait_recv()

            def body(b, carry):
                s3[h, b, rows, lanes] = (
                    part[h, b, rows, lanes] + r1[h, b, rows, lanes].astype(F32)
                ).astype(BF)
                return carry

            lax.fori_loop(0, NB, body, 0)
            live["t3", k, h] = start(
                k, 4 + h, s3.at[h, :, rows, lanes], r3.at[h, :, rows, lanes], dev(dx=1 if h == 0 else 3)
            )

    def t4(k):
        rows, lanes = cut(k)
        for h in range(2):
            live["t2", k, h].wait_recv()
            live["t3", k, h].wait_recv()

        def body(b, carry):
            s4[b, rows, lanes] = (
                part[2 + ozh, b, rows, lanes]
                + r2[ozh, b, rows, lanes].astype(F32)
                + r3[ozh, b, rows, lanes].astype(F32)
            ).astype(BF)
            return carry

        lax.fori_loop(0, NB, body, 0)
        live["t4", k] = start(k, 6, s4.at[:, rows, lanes], r4.at[:, rows, lanes], dev(dh=1))

    corr_one = 1.0 - 0.9**INNER_STEP
    corr_two = 1.0 - 0.95**INNER_STEP

    def t5(k):
        rows, lanes = cut(k)
        live["t4", k].wait_recv()

        def body(b, carry):
            grad = (
                part[2 + zh, b, rows, lanes]
                + r2[zh, b, rows, lanes].astype(F32)
                + r3[zh, b, rows, lanes].astype(F32)
                + r4[b, rows, lanes].astype(F32)
            ) * (1.0 / 8192.0)
            one = 0.9 * st_t[1, b, rows, lanes] + 0.1 * grad
            two = 0.95 * st_t[2, b, rows, lanes] + 0.05 * grad * grad
            step = (one * (0.02 / corr_one)) / (jnp.sqrt(two * (1.0 / corr_two)) + 1e-08)
            s5[b, rows, lanes] = st_t[3, b, rows, lanes] - (st_t[0, b, rows, lanes] - step)
            return carry

        lax.fori_loop(0, NB, body, 0)
        for d in (1, 2, 3):
            live["t5", k, d] = start(
                k, 6 + d, s5.at[lax.rem(y + d, 4), rows, lanes], r5.at[d - 1, rows, lanes], dev(dy=d)
            )

    def t6(k):
        rows, lanes = cut(k)
        for d in (1, 2, 3):
            live["t5", k, d].wait_recv()
        total = s5[y, rows, lanes]
        for d in range(3):
            total += r5[d, rows, lanes]
        slot = zh * 4 + zl
        r6[slot, rows, lanes] = total.astype(BF)
        ref = r6.at[slot, rows, lanes]
        for d in (1, 2, 3):
            live["t6", k, d] = start(k, 9 + d, ref, ref, dev(dl=d))
        if k in WIDE:
            for d in range(4):
                live["t6", k, 4 + d] = start(k, 40 + d, ref, ref, dev(dl=d, dh=1))

    def parts_of(k):
        r0, rn, l0, ln = CHUNKS[k]
        return (pl.ds(r0, FIRST[k]), pl.ds(r0 + FIRST[k], rn - FIRST[k])), pl.ds(l0, ln)

    def gather_one(k, other):
        (first, second), lanes = parts_of(k)
        h = ozh if other else zh
        for d in (1, 2, 3):
            ref = w_v.at[c, h, x, y, first, lanes]
            live["mid", k, other, 0, d] = start(k, 13 + 6 * other + d, ref, ref, dev(dx=d))
            ref = w_v.at[c, h, x, y, second, lanes]
            live["mid", k, other, 1, d] = start(k, 16 + 6 * other + d, ref, ref, dev(dy=d))

    def t7(k):
        rows, lanes = cut(k)
        for d in (1, 2, 3):
            live["t6", k, d].wait_recv()
        if k in WIDE:
            for d in range(4):
                live["t6", k, 4 + d].wait_recv()

        def average(h):
            total = r6[h * 4, rows, lanes].astype(F32)
            for m in range(1, 4):
                total += r6[h * 4 + m, rows, lanes].astype(F32)
            return total * (1.0 / 16.0)

        mean = average(zh)
        moment = 0.9 * st_t[4, y, rows, lanes] + mean
        fresh = st_t[3, y, rows, lanes] - 0.7 * (mean + 0.9 * moment)
        w_v[c, zh, x, y, rows, lanes] = fresh.astype(BF)
        if k in WIDE:
            if "base" in live:
                live.pop("base").wait_recv()
            w_v[c, ozh, x, y, rows, lanes] = (base_c[1, rows, lanes] - 1.33 * average(ozh)).astype(BF)
            ref = w_v.at[c, :, x, y, rows, lanes]
            for d in DIRECT:
                live["all", k, d] = start(k, 13 + d, ref, ref, dev(dx=d % 4, dy=d // 4))
        else:
            ref = w_v.at[c, zh, x, y, rows, lanes]
            live["t7", k] = start(k, 13, ref, ref, dev(dh=1))
            gather_one(k, 0)
        nb_v[rows, lanes] = fresh
        nm_v[rows, lanes] = moment

    def t7b(k):
        live["t7", k].wait_recv()
        gather_one(k, 1)

    def gather_two(k, other):
        (first, second), lanes = parts_of(k)
        h = ozh if other else zh
        for p in range(2):
            for d in (1, 2, 3):
                live["mid", k, other, p, d].wait_recv()
            ref = w_v.at[c, h, :, y, first, lanes] if p == 0 else w_v.at[c, h, x, :, second, lanes]
            for d in (1, 2, 3):
                live["end", k, other, p, d] = start(
                    k, 25 + 6 * other + 3 * p + d, ref, ref, dev(dy=d) if p == 0 else dev(dx=d)
                )

    def gather_three(k, other):
        rows, lanes = cut(k)
        for p in range(2):
            for d in (1, 2, 3):
                live["end", k, other, p, d].wait_recv()
        ref = w_v.at[c, ozh if other else zh, :, :, rows, lanes]
        live["core", k, other] = start(k, 38 + other, ref, ref, dev(dc=1))

    def gather_all(k):
        rows, lanes = cut(k)
        for d in DIRECT:
            live["all", k, d].wait_recv()
        ref = w_v.at[c, :, :, :, rows, lanes]
        live["core", k, 0] = start(k, 38, ref, ref, dev(dc=1))

    def t10(k):
        live["core", k, 0].wait_recv()
        if k not in WIDE:
            live["core", k, 1].wait_recv()

    def give(n, h):
        give_mul(n, h)
        give_send(n, h)

    def mul_a():
        load_acts.wait()
        give_mul(0, 0)
        give_mul(0, 1)
        load(2)
        load(3)
        pl.semaphore_wait(bar, len(peers))
        give_send(0, 0, 0)
        give_send(0, 1, 0)
        load_states()
        give(1, 1)
        give(2, 0)
        for h in range(2):
            keep(0, h, s1.at[h], 0)
            for k in range(3):
                t1(k, (h,))
        give(1, 0)
        give(2, 1)
        give_send(0, 0, 1)
        give_send(0, 1, 1)
        keep(1, 1, s2.at[1])
        keep(2, 0, s2.at[0])
        t2(0)
        give(3, 0)
        give(3, 1)

    def mul_b():
        keep(1, 0, part.at[0])
        keep(2, 1, part.at[1])

    def mul_c():
        keep(0, 0, s1.at[0], 1)
        keep(0, 1, s1.at[1], 1)

    def mul_d():
        keep(3, 0, part.at[2])
        keep(3, 1, part.at[3])

    def stage_rest():
        for cp in states:
            cp.wait()
        mine = st_t[3, y, WIDE_ROWS, WIDE_LANES] - 0.567 * st_t[4, y, WIDE_ROWS, WIDE_LANES]
        base_c[0, WIDE_ROWS, WIDE_LANES] = mine
        live["base"] = remote(
            base_c.at[0, WIDE_ROWS, WIDE_LANES], base_c.at[1, WIDE_ROWS, WIDE_LANES], bs_sem, br_sem, dev(dh=1)
        )
        live["base"].start()
        pending.append(live["base"])
        na_v[...] = na_t[...].T

    def product(p, hh):
        for xx in range(0, 4, 2):
            pair = jnp.concatenate(
                [w_v[p, hh, xx + m, :, :, :128].reshape(NB * RB, 128) for m in range(2)], axis=1
            )
            half_v[p, hh, xx // 2] = jnp.dot(na_v[...], pair, preferred_element_type=F32).astype(BF)

    done = []

    def drain(keep_last):
        n = len(pending) - keep_last
        for cp in pending[len(done) : n]:
            cp.wait_send()
            done.append(cp)

    steps = [
        (mul_a,), (mul_b,), (t3, 0), (t3, 1), (stage_rest,), (t2, 1), (t2, 2), (t3, 2), (mul_c,), (mul_d,),
        (t4, 0), (t4, 1), (t1, 3), (t5, 0), (t1, 6), (t4, 2), (t2, 3), (t3, 3), (t1, 4), (t2, 4), (t5, 1),
        (t6, 0), (t4, 3), (t3, 4), (t6, 1), (t5, 2), (t2, 6), (t7, 0), (drain, 40), (t1, 5), (t3, 6), (t2, 5),
        (t4, 4), (t6, 2), (t3, 5), (t5, 3), (t7, 1), (t4, 6), (gather_two, 0, 0), (t5, 4), (t4, 5), (t7b, 0),
        (gather_two, 1, 0), (t7, 2), (drain, 40), (t6, 3), (t7b, 1), (t5, 6), (gather_two, 0, 1), (t6, 4),
        (t5, 5), (gather_two, 1, 1), (t6, 6), (t7b, 2), (gather_two, 2, 0), (t7, 3), (gather_three, 1, 0),
        (t7, 4), (t6, 5), (gather_two, 2, 1), (gather_three, 0, 1), (t7, 6), (drain, 60), (gather_three, 0, 0),
        (t7b, 3), (gather_two, 3, 0), (gather_three, 1, 1), (t7b, 4), (gather_two, 4, 0), (gather_three, 2, 1),
        (gather_three, 2, 0), (t7, 5), (drain, 60), (gather_two, 4, 1), (t10, 0), (gather_three, 3, 0),
        (gather_two, 3, 1), (t10, 1), (gather_all, 6), (t10, 6), (t10, 2), (gather_all, 5), (gather_three, 4, 1),
        (gather_three, 4, 0), (gather_three, 3, 1), (product, 0, 0), (product, 0, 1), (product, 1, 0), (t10, 5),
        (product, 1, 1), (t10, 3), (t10, 4),
    ]
    for step in steps:
        step[0](*step[1:])
    for cp in swaps.values():
        cp.wait_send()
    drain(0)


def project_kernel(a_ref, w_ref, nb_ref, nm_ref, half_ref, o_ref, nbo_ref, nmo_ref):
    step = pl.program_id(0)
    hh, pr = step // 2, lax.rem(step, 2)
    for p in range(2):
        pair = jnp.concatenate(
            [w_ref[p, hh, pr * 2 + m, :, :, 128:].reshape(NB * RB, 128) for m in range(2)], axis=1
        )
        out = jnp.dot(a_ref[...], pair, preferred_element_type=F32).astype(BF)
        for m in range(2):
            lo = (m * 2 + p) * 256
            o_ref[:, lo : lo + 128] = half_ref[p, hh, pr, :, m * 128 : (m + 1) * 128]
            o_ref[:, lo + 128 : lo + 256] = out[:, m * 128 : (m + 1) * 128]
    zl = lax.rem(lax.axis_index("island"), 4)

    @pl.when(step == 0)
    def _():
        for k in range(4):
            @pl.when(zl == k)
            def _():
                nbo_ref[...] = nb_ref[pl.ds(52 * k, 52), :]
                nmo_ref[...] = nm_ref[pl.ds(52 * k, 52), :]


def per_device(
    acts, grad_out, next_acts, inner_params, adam_first, adam_second, base_params, outer_moment
):
    n = len(CHUNKS)
    dma, vm = pltpu.SemaphoreType.DMA, pltpu.VMEM
    hbm = pl.BlockSpec(memory_space=pl.ANY)
    block = (NB, RB, 256)
    acts_tr = acts.T.reshape(NB, RB, 512)
    states = [a[0].T.reshape(block) for a in (inner_params, adam_first, adam_second)]
    states += [a.T.reshape(block) for a in (base_params, outer_moment)]
    w, nb, nm, na, half = pl.pallas_call(
        comm_kernel,
        out_shape=(
            vm((2, 2, 4) + block, BF), vm((RB, 256), F32), vm((RB, 256), F32), vm((512, 832), BF),
            vm((2, 2, 2, 512, 256), BF),
        ),
        in_specs=[hbm] * 8,
        out_specs=(pl.BlockSpec(memory_space=vm),) * 5,
        scratch_shapes=[
            vm((NB, RB, 512), BF), vm((4, 2, 2, 512, 256), BF), vm((4, 2) + block, BF), vm((4, 2) + block, BF),
            vm((4,) + block, F32),
            vm((2,) + block, BF), vm((2,) + block, BF), vm((2,) + block, BF), vm((2,) + block, BF),
            vm((2,) + block, BF), vm((2,) + block, BF), vm(block, BF), vm(block, BF), vm(block, F32),
            vm((3, RB, 256), F32), vm((8, RB, 256), BF),
            vm((5,) + block, F32), vm((832, 512), BF), vm((2, RB, 256), F32),
            dma((7,)), dma((4, 2, 2)), dma((4, 2, 2)), dma((4, 2, 2)), dma, dma, dma((n, 44)), dma((n, 44)),
        ],
        compiler_params=pltpu.CompilerParams(
            collective_id=0, has_side_effects=True, vmem_limit_bytes=48 * 2**20
        ),
        name="outer_round",
    )(acts_tr, grad_out, *states, next_acts.T)
    whole = pl.BlockSpec(memory_space=vm)
    small = pl.BlockSpec((52, 256), lambda i: (0, 0))
    next_out, base_out, moment_out = pl.pallas_call(
        project_kernel,
        grid=(4,),
        out_shape=(
            jax.ShapeDtypeStruct((512, 4096), BF),
            jax.ShapeDtypeStruct((52, 256), F32),
            jax.ShapeDtypeStruct((52, 256), F32),
        ),
        in_specs=[
            whole,
            whole,
            whole,
            whole,
            whole,
        ],
        out_specs=(pl.BlockSpec((512, 1024), lambda i: (0, i)), small, small),
        compiler_params=pltpu.CompilerParams(vmem_limit_bytes=24 * 2**20),
        name="project",
    )(na, w, nb, nm, half)
    return base_out.T, moment_out.T, next_out


def solution(mesh):
    in_specs = (
        P(("island", "fsdp"), None),
        P(("island", "fsdp"), None),
        P(("island", "fsdp"), None),
        P("island", "fsdp", None),
        P("island", "fsdp", None),
        P("island", "fsdp", None),
        P("fsdp", None),
        P("fsdp", None),
    )
    out_specs = (P("fsdp", "island"), P("fsdp", "island"), P(("island", "fsdp"), None))
    return jax.shard_map(
        per_device, mesh=mesh, in_specs=in_specs, out_specs=out_specs, check_vma=False
    )
```
